128 devices in a mesh: dp: 16 (over z, y), section: 8 (over x, core).
Axes of the slice: x: 4, y: 4, z: 4, core: 2. Of those that a mesh axis runs over, the one named last changes fastest.
Arguments:
- queries: bfloat16 [8, 98304, 128], P(None, ('dp', 'section')), may hold values from -6 to 6
- grad_out: bfloat16 [8, 98304, 128], P(None, ('dp', 'section')), may hold values from -24 to 24
- log_norm: bfloat16 [8, 98304], P(None, ('dp', 'section')), may hold values from 2 to 10
- row_delta: bfloat16 [8, 98304], P(None, ('dp', 'section')), may hold values from -24 to 24
- key_rows: bfloat16 [98304, 128], P(('dp', 'section')), may hold values from -6 to 6
- value_rows: bfloat16 [98304, 128], P(('dp', 'section')), may hold values from -6 to 6
- doc_lengths: int32 [256], replicated, may hold values from 1 to 3072, as said below
Outputs:
- query_grad: bfloat16 [8, 98304, 128], P(None, ('dp', 'section'))
- key_grad: bfloat16 [98304, 128], P(('dp', 'section'))
- value_grad: bfloat16 [98304, 128], P(('dp', 'section'))
The draws below stay inside these ranges and needn't reach their ends.
Inputs may be any that keep to these rules, and one draw needn't show every extreme that they name: `doc_lengths`: 256 document lengths in packing order that sum to 98304; the longest is exactly 3072.
All inputs are finite; a program needn't handle non-finite values.
Results may differ from the reference program's by a relative error of at most 0.0012.
The reference program's roundings to bfloat16 on the way (of `probs_rounded` and `grads_rounded`) count: a program that leaves them out, or rounds other values in their place, can miss the bound.
Values may be sent and summed in bfloat16 or wider, within the bound.
A program may use at most 192 MiB of HBM per device.

```python
import math
import jax
import jax.numpy as jnp
from jax import lax

D = 128
HQ = 8
TOK_DEV = 768
REACH = 4
TOKENS = 98304
MAXDOC = 3072
NDOC = 256


def document_lengths(key):
    others = NDOC - 1
    remaining = TOKENS - MAXDOC
    spare_tokens = remaining - others
    powers = jax.random.randint(jax.random.fold_in(key, 101), (others,), 0, 4, dtype=jnp.int32)
    weights = jnp.left_shift(jnp.ones((others,), jnp.int32), powers)
    weight_total = jnp.sum(weights).astype(jnp.int32)
    lengths = (1 + weights * spare_tokens // weight_total).astype(jnp.int32)
    deficit = (remaining - jnp.sum(lengths)).astype(jnp.int32)
    lengths = lengths + (jnp.arange(others, dtype=jnp.int32) < deficit).astype(jnp.int32)
    lengths = jnp.concatenate([jnp.full((1,), MAXDOC, jnp.int32), lengths.astype(jnp.int32)])
    shuffle = jax.random.permutation(jax.random.fold_in(key, 102), NDOC)
    return lengths[shuffle].astype(jnp.int32)


def draw_doc_lengths(key, part):
    lengths = document_lengths(key)
    return lengths


def draw_log_norm(key, part):
    lengths = document_lengths(key)
    key = jax.random.fold_in(key, 7)
    doc_ends = jnp.cumsum(lengths).astype(jnp.int32)
    positions = jnp.arange(TOKENS, dtype=jnp.int32)
    doc_ids = jnp.searchsorted(doc_ends, positions, side='right').astype(jnp.int32)
    starts = (doc_ends - lengths)[doc_ids]
    offset_in_doc = (positions - starts).astype(jnp.float32)
    jitter = jax.random.uniform(key, (HQ, TOKENS), jnp.float32, 0.0, 1.0)
    return (jnp.log(offset_in_doc + 16.0)[None, :] + jitter).astype(jnp.bfloat16)


def steps_of(key, extent, split, smallest, largest):
    def one(dim, blocks):
        steps = jax.random.uniform(jax.random.fold_in(jax.random.fold_in(key, 6), dim), (blocks,), jnp.float32, smallest / len(split), largest / len(split))
        return jnp.repeat(jnp.exp(steps), extent[dim] // blocks).reshape((-1,) + (1,) * (len(extent) - dim - 1))

    loudness = one(*split[0])
    for cut in split[1:]:
        loudness = loudness * one(*cut)
    return loudness


def noise(key, shape, scale, bound, shards=(), kind=jnp.bfloat16):
    entries = jax.random.normal(key, shape, jnp.float32) * scale
    if len(shards) > 0:
        entries = steps_of(key, shape, shards, -0.22, 0.18) * entries
    return jnp.clip(entries, min=-bound, max=bound).astype(kind)


def setup_inputs(seed: int = 0) -> dict:
    seeds = jax.random.split(jax.random.key(seed), 8)
    return {
        "queries": noise(seeds[0], (HQ, TOKENS, D), 1.0, 6.0, ((1, 128),)),
        "grad_out": noise(seeds[1], (HQ, TOKENS, D), 4.0, 24.0, ((1, 128),)),
        "log_norm": draw_log_norm(jax.random.fold_in(seeds[7], 71), 0),
        "row_delta": noise(seeds[3], (HQ, TOKENS), 4.0, 24.0, ((1, 128),)),
        "key_rows": noise(seeds[4], (TOKENS, D), 1.0, 6.0, ((0, 128),)),
        "value_rows": noise(seeds[5], (TOKENS, D), 1.0, 6.0, ((0, 128),)),
        "doc_lengths": draw_doc_lengths(jax.random.fold_in(seeds[7], 71), 0),
    }


def document_of(positions, doc_ends):
    passed = lax.optimization_barrier(jnp.sum((positions[:, None] >= doc_ends[None, :]).astype(jnp.int32), axis=1))
    return jnp.where(positions < 0, -1, passed).astype(jnp.int32)

def reference(queries, grad_out, log_norm, row_delta, key_rows, value_rows, doc_lengths):
    score_scale = 1.0 / math.sqrt(D)
    doc_ends = jnp.cumsum(doc_lengths).astype(jnp.int32)
    reach_rows = REACH * TOK_DEV
    window_rows = reach_rows + TOK_DEV
    key_padded = jnp.concatenate([jnp.zeros((reach_rows, D), key_rows.dtype), key_rows], axis=0)
    value_padded = jnp.concatenate([jnp.zeros((reach_rows, D), value_rows.dtype), value_rows], axis=0)

    def block_step(totals, block_index):
        key_grads, value_grads = totals
        row_start = (block_index * TOK_DEV).astype(jnp.int32)
        query_block = lax.dynamic_slice_in_dim(queries, row_start, TOK_DEV, 1).astype(jnp.float32)
        grad_block = lax.dynamic_slice_in_dim(grad_out, row_start, TOK_DEV, 1).astype(jnp.float32)
        norm_block = lax.dynamic_slice_in_dim(log_norm, row_start, TOK_DEV, 1).astype(jnp.float32)
        delta_block = lax.dynamic_slice_in_dim(row_delta, row_start, TOK_DEV, 1).astype(jnp.float32)
        key_block = lax.dynamic_slice_in_dim(key_padded, row_start, window_rows, 0).astype(jnp.float32)
        value_block = lax.dynamic_slice_in_dim(value_padded, row_start, window_rows, 0).astype(jnp.float32)
        query_pos = row_start + jnp.arange(TOK_DEV, dtype=jnp.int32)
        key_pos = row_start - reach_rows + jnp.arange(window_rows, dtype=jnp.int32)
        query_doc = document_of(query_pos, doc_ends)
        key_doc = document_of(key_pos, doc_ends)
        allowed = (query_doc[:, None] == key_doc[None, :]) & (key_pos[None, :] <= query_pos[:, None])
        scores = jnp.einsum('hrd,cd->hrc', query_block, key_block) * score_scale
        attn_probs = jnp.exp(jnp.where(allowed[None], scores - norm_block[:, :, None], -1e+30))
        prob_grads = jnp.einsum('hrd,cd->hrc', grad_block, value_block)
        score_grads = attn_probs * (prob_grads - delta_block[:, :, None])
        probs_rounded = lax.optimization_barrier(attn_probs.astype(jnp.bfloat16)).astype(jnp.float32)
        grads_rounded = lax.optimization_barrier(score_grads.astype(jnp.bfloat16)).astype(jnp.float32)
        value_part = jnp.einsum('hrc,hrd->cd', probs_rounded, grad_block)
        key_part = jnp.einsum('hrc,hrd->cd', grads_rounded, query_block) * score_scale
        query_part = jnp.einsum('hrc,cd->hrd', grads_rounded, key_block) * score_scale
        old_keys = lax.dynamic_slice_in_dim(key_grads, row_start, window_rows, 0)
        key_grads = lax.dynamic_update_slice_in_dim(key_grads, old_keys + key_part, row_start, 0)
        old_values = lax.dynamic_slice_in_dim(value_grads, row_start, window_rows, 0)
        value_grads = lax.dynamic_update_slice_in_dim(value_grads, old_values + value_part, row_start, 0)
        return ((key_grads, value_grads), query_part.astype(jnp.bfloat16))
    start_totals = (jnp.zeros((TOKENS + reach_rows, D), jnp.float32), jnp.zeros((TOKENS + reach_rows, D), jnp.float32))
    block_ids = jnp.arange(TOKENS // TOK_DEV, dtype=jnp.int32)
    (key_grads, value_grads), blocks = lax.scan(block_step, start_totals, block_ids)
    query_grad = jnp.transpose(blocks, (1, 0, 2, 3)).reshape(HQ, TOKENS, D)
    key_grad = key_grads[reach_rows:].astype(jnp.bfloat16)
    value_grad = value_grads[reach_rows:].astype(jnp.bfloat16)
    return (query_grad, key_grad, value_grad)
```

```python
import functools
import math

import jax
import jax.numpy as jnp
from jax import lax
from jax.experimental import pallas as pl
from jax.experimental.pallas import tpu as pltpu
from jax.sharding import PartitionSpec as P

AXES = ("dp", "section")
REACH = 4
CHUNK = 256
DIGIT = 16
MASKED = 32768.0
LOG2E = 1.4426950408889634
MESH = pl.DeviceIdType.MESH

NN = (((1,), (0,)), ((), ()))
NT = (((1,), (1,)), ((), ()))
dot = functools.partial(lax.dot_general, preferred_element_type=jnp.float32)

ORDER = (
    ((0, 1), (), ()),
    ((0, 2), (), (("kv", 1),)),
    ((1, 0), (), ()),
    ((1, 1), (), ()),
    ((1, 2), (), (("kv", 2),)),
    ((2, 0), (), ()),
    ((2, 1), (), (("kv", 3),)),
    ((3, 0), (), (("kv", 4),)),
    ((4, 2), (), ()),
    ((4, 1), (("ret", 4, 2),), ()),
    ((4, 0), (("ret", 4, 1),), ()),
    ((3, 1), (("ret", 4, 0),), ()),
    ((3, 2), (("ret", 3, 0), ("ret", 3, 1)), ()),
    ((2, 2), (("ret", 3, 2), ("ret", 2, 0)), ()),
    ((0, 0), (("ret", 2, 1), ("ret", 2, 2), ("ret", 1, 0)), ()),
    (None, (("ret", 1, 1), ("ret", 1, 2)), ()),
)


def rows_of(offset, chunk, rows):
    if offset == 0:
        return chunk * CHUNK, rows
    if offset == REACH:
        return 0, (chunk + 1) * CHUNK
    return 0, rows


def kernel(
    count, sections, scale,
    q_in, g_in, norm_in, delta_in, k_in, v_in, lens_in,
    dq_out, dk_out, dv_out,
    qa, ga, qt, gt, kv, ka, va, dq, part, got, probs, grads, stat, base, ends,
    q_sem, g_sem, own_sem, kv_send, kv_recv, part_send, part_recv,
):
    heads, rows, width = dq.shape
    chunks = rows // CHUNK
    f32, b16 = jnp.float32, jnp.bfloat16
    me = lax.axis_index("dp") * sections + lax.axis_index("section")
    right = lax.rem(me + 1, count)
    left = lax.rem(me + count - 1, count)
    right = (right // sections, lax.rem(right, sections))
    left = (left // sections, lax.rem(left, sections))

    def load_q(h):
        return pltpu.make_async_copy(q_in.at[h], qa.at[h, :, pl.ds(0, width)], q_sem.at[h])

    def load_g(h):
        return pltpu.make_async_copy(g_in.at[h], ga.at[h, :, pl.ds(0, width)], g_sem.at[h])

    own = [pltpu.make_async_copy(ref, kv.at[0, j], own_sem.at[j]) for j, ref in enumerate((k_in, v_in))]
    for copy in own:
        copy.start()

    def start_loads(h, carry):
        load_q(h).start()
        load_g(h).start()
        return carry

    lax.fori_loop(0, heads, start_loads, 0)

    barrier = pltpu.get_barrier_semaphore()
    for neighbour in (left, right):
        pl.semaphore_signal(barrier, inc=1, device_id=neighbour, device_id_type=MESH)

    def pass_on(offset):
        return [
            pltpu.make_async_remote_copy(
                src_ref=(k_in, v_in)[j] if offset == 0 else kv.at[offset, j],
                dst_ref=kv.at[offset + 1, j],
                send_sem=kv_send.at[offset, j],
                recv_sem=kv_recv.at[offset, j],
                device_id=right,
                device_id_type=MESH,
            )
            for j in range(2)
        ]

    def hand_back(offset, chunk):
        return pltpu.make_async_remote_copy(
            src_ref=part.at[offset, chunk],
            dst_ref=got.at[offset - 1, chunk],
            send_sem=part_send.at[offset - 1, chunk],
            recv_sem=part_recv.at[offset - 1, chunk],
            device_id=left,
            device_id_type=MESH,
        )

    pl.semaphore_wait(barrier, 2)
    for copy in pass_on(0):
        copy.start()

    line = lax.broadcasted_iota(jnp.int32, (256, 256), 0)
    lane = lax.broadcasted_iota(jnp.int32, (256, 256), 1)
    lens = lens_in[...].astype(f32)
    ends[...] = jnp.sum(jnp.where(lane <= line, lens, 0.0), axis=1, keepdims=True)
    row = lax.broadcasted_iota(jnp.int32, (width, rows), 0)
    rowf = row.astype(f32)
    place = lax.broadcasted_iota(jnp.int32, (1, rows), 1)

    def matches(offset):
        first = lax.rem(me + count - offset, count) * rows
        where = (first + place).astype(f32)
        number = jnp.sum(jnp.where(ends[...] <= where, 1.0, 0.0), axis=0, keepdims=True)
        high = jnp.floor(number * (1.0 / DIGIT))
        low = number - high * DIGIT + DIGIT
        return (rowf == high) | (rowf == low)

    def key_side(offset):
        blocked = jnp.where(matches(offset), 0.0, -MASKED)
        ones = jnp.where(row < 2 * DIGIT + 3, 1.0, 0.0)
        ka[offset, :, width:] = jnp.where(row < 2 * DIGIT, blocked, ones).astype(b16).T
        va[offset, :, width:] = jnp.where(row < 1, 1.0, 0.0).astype(b16).T

    def take_keys(offset):
        ka[offset, :, :width] = kv[offset, 0]
        va[offset, :, :width] = kv[offset, 1]

    base[...] = jnp.where(matches(0), 1.0, 0.0)
    stat[0] = norm_in[...].astype(f32) * (-1.0 / scale)
    stat[1] = -delta_in[...].astype(f32)

    def prepare(h, carry):
        norm = stat[0, pl.ds(h, 1), :]
        high = norm.astype(b16).astype(f32)
        middle = (norm - high).astype(b16).astype(f32)
        low = norm - high - middle
        extra = jnp.where(
            row == 2 * DIGIT,
            high,
            jnp.where(row == 2 * DIGIT + 1, middle, jnp.where(row == 2 * DIGIT + 2, low, base[...])),
        )
        qa[h, :, width:] = extra.astype(b16).T
        ga[h, :, width:] = jnp.where(row == 0, stat[1, pl.ds(h, 1), :], 0.0).astype(b16).T
        load_q(h).wait()
        load_g(h).wait()
        qt[h] = qa[h, :, :width].T
        gt[h] = ga[h, :, :width].T
        dq[h] = jnp.zeros((rows, width), f32)
        return carry

    lax.fori_loop(0, heads, prepare, 0)
    for offset in range(REACH + 1):
        key_side(offset)
    for copy in own:
        copy.wait()
    take_keys(0)
    part[...] = jnp.zeros_like(part)

    def first_half(offset, chunk, h, slot):
        low, high = rows_of(offset, chunk, rows)
        keys = slice(chunk * CHUNK, (chunk + 1) * CHUNK)
        scores = dot(qa[h, low:high, :], ka[offset, keys, :], NT)
        if offset == 0:
            i = lax.broadcasted_iota(jnp.int32, scores.shape, 0)
            j = lax.broadcasted_iota(jnp.int32, scores.shape, 1)
            scores = jnp.where(j <= i, scores, -1e30)
        p = jnp.exp2(scores * (scale * LOG2E))
        ds = p * dot(ga[h, low:high, :], va[offset, keys, :], NT)
        probs[slot, low:high, :] = p.astype(b16)
        grads[slot, low:high, :] = ds.astype(b16)

    def second_half(offset, chunk, h, slot):
        low, high = rows_of(offset, chunk, rows)
        keys = slice(chunk * CHUNK, (chunk + 1) * CHUNK)
        p = probs[slot, low:high, :]
        ds = grads[slot, low:high, :]
        part[offset, chunk, 0] += dot(qt[h, :, low:high], ds, NN)
        part[offset, chunk, 1] += dot(gt[h, :, low:high], p, NN)
        dq[h, low:high, :] += dot(ds, kv[offset, 0, keys, :], NN)

    def act(event):
        if event[0] == "kv":
            offset = event[1]
            for copy in pass_on(offset - 1):
                copy.wait_recv()
            if offset < REACH:
                for copy in pass_on(offset):
                    copy.start()
            take_keys(offset)
        else:
            _, offset, chunk = event
            if offset < REACH:
                hand_back(offset + 1, chunk).wait_recv()
                part[offset, chunk] += got[offset, chunk]
            hand_back(offset, chunk).start()

    first_half(*ORDER[0][0], 0, 0)
    for n, (item, at_start, ahead) in enumerate(ORDER):
        for event in at_start:
            act(event)
        if item is None:
            break

        def pair(j, carry, item=item):
            first_half(*item, 2 * j + 1, 1)
            second_half(*item, 2 * j, 0)
            first_half(*item, 2 * j + 2, 0)
            second_half(*item, 2 * j + 1, 1)
            return carry

        lax.fori_loop(0, heads // 2 - 1, pair, 0)
        for event in ahead:
            act(event)
        first_half(*item, heads - 1, 1)
        second_half(*item, heads - 2, 0)
        if ORDER[n + 1][0] is not None:
            first_half(*ORDER[n + 1][0], 0, 0)
        second_half(*item, heads - 1, 1)

    def finish(h, carry):
        dq_out[h] = (dq[h] * scale).astype(b16)
        return carry

    lax.fori_loop(0, heads, finish, 0)
    for chunk in range(chunks):
        keys = slice(chunk * CHUNK, (chunk + 1) * CHUNK)
        hand_back(1, chunk).wait_recv()
        dk_out[keys, :] = ((part[0, chunk, 0] + got[0, chunk, 0]) * scale).T.astype(b16)
        dv_out[keys, :] = (part[0, chunk, 1] + got[0, chunk, 1]).T.astype(b16)
    for offset in range(REACH):
        for copy in pass_on(offset):
            copy.wait_send()
        for chunk in range(chunks):
            hand_back(offset + 1, chunk).wait_send()


def per_device(count, sections, queries, grad_out, log_norm, row_delta, key_rows, value_rows, doc_lengths):
    heads, rows, width = queries.shape
    chunks = rows // CHUNK
    scale = 1.0 / math.sqrt(width)
    f32, b16 = jnp.float32, jnp.bfloat16
    vmem = pl.BlockSpec(memory_space=pltpu.VMEM)
    anywhere = pl.BlockSpec(memory_space=pl.ANY)
    dma = pltpu.SemaphoreType.DMA
    blocks = heads * rows * (REACH + 1 - 1) * rows
    return pl.pallas_call(
        functools.partial(kernel, count, sections, scale),
        out_shape=(
            jax.ShapeDtypeStruct((heads, rows, width), b16),
            jax.ShapeDtypeStruct((rows, width), b16),
            jax.ShapeDtypeStruct((rows, width), b16),
        ),
        in_specs=[anywhere, anywhere, vmem, vmem, anywhere, anywhere, vmem],
        out_specs=(vmem, vmem, vmem),
        scratch_shapes=[
            pltpu.VMEM((heads, rows, 2 * width), b16),
            pltpu.VMEM((heads, rows, 2 * width), b16),
            pltpu.VMEM((heads, width, rows), b16),
            pltpu.VMEM((heads, width, rows), b16),
            pltpu.VMEM((REACH + 1, 2, rows, width), b16),
            pltpu.VMEM((REACH + 1, rows, 2 * width), b16),
            pltpu.VMEM((REACH + 1, rows, 2 * width), b16),
            pltpu.VMEM((heads, rows, width), f32),
            pltpu.VMEM((REACH + 1, chunks, 2, width, CHUNK), f32),
            pltpu.VMEM((REACH, chunks, 2, width, CHUNK), f32),
            pltpu.VMEM((2, rows, CHUNK), b16),
            pltpu.VMEM((2, rows, CHUNK), b16),
            pltpu.VMEM((2, heads, rows), f32),
            pltpu.VMEM((width, rows), f32),
            pltpu.VMEM((256, 1), f32),
            dma((heads,)),
            dma((heads,)),
            dma((2,)),
            dma((REACH, 2)),
            dma((REACH, 2)),
            dma((REACH, chunks)),
            dma((REACH, chunks)),
        ],
        compiler_params=pltpu.CompilerParams(
            collective_id=0, has_side_effects=True, vmem_limit_bytes=56 * 1024 * 1024
        ),
        cost_estimate=pl.CostEstimate(
            flops=10 * blocks * width, bytes_accessed=8 * heads * rows * width, transcendentals=blocks
        ),
        name="packed_attention_grads",
    )(queries, grad_out, log_norm, row_delta, key_rows, value_rows, doc_lengths.reshape(1, -1))


def solution(mesh):
    placed = (
        P(None, AXES, None),
        P(None, AXES, None),
        P(None, AXES),
        P(None, AXES),
        P(AXES, None),
        P(AXES, None),
        P(),
    )
    return jax.shard_map(
        functools.partial(per_device, mesh.size, mesh.shape["section"]),
        mesh=mesh,
        in_specs=placed,
        out_specs=(P(None, AXES, None), P(AXES, None), P(AXES, None)),
        check_vma=False,
    )
```

```python
import functools
import math

import jax
import jax.numpy as jnp
from jax import lax
from jax.experimental import pallas as pl
from jax.experimental.pallas import tpu as pltpu
from jax.sharding import PartitionSpec as P

AXES = ("dp", "section")
REACH = 4
CHUNK = 256
DIGIT = 16
STEPS = 14.0
EXACT = 0.5
MASKED = 32768.0
LOG2E = 1.4426950408889634
MESH = pl.DeviceIdType.MESH

NN = (((1,), (0,)), ((), ()))
NT = (((1,), (1,)), ((), ()))
dot = functools.partial(lax.dot_general, preferred_element_type=jnp.float32)

ORDER = (
    ((0, 1), {}),
    ((0, 2), {3: (("kv", 1),)}),
    ((1, 0), {}),
    ((1, 1), {3: (("kv", 2),)}),
    ((1, 2), {}),
    ((2, 0), {2: (("kv", 3),)}),
    ((2, 1), {3: (("kv", 4),)}),
    ((4, 2), {}),
    ((4, 1), {0: (("ret", 4, 2),)}),
    ((4, 0), {0: (("ret", 4, 1),)}),
    ((3, 2), {0: (("ret", 4, 0),)}),
    ((3, 1), {0: (("ret", 3, 2),)}),
    ((3, 0), {0: (("ret", 3, 1),)}),
    ((2, 2), {0: (("ret", 3, 0), ("ret", 2, 1)), 3: (("ret", 2, 0),)}),
    ((0, 0), {0: (("ret", 2, 2), ("ret", 1, 1)), 3: (("ret", 1, 0),)}),
    (None, {0: (("ret", 1, 2),)}),
)


def rows_of(offset, chunk, rows):
    if offset == 0:
        return chunk * CHUNK, rows
    if offset == REACH:
        return 0, (chunk + 1) * CHUNK
    return 0, rows


def kernel(
    count, sections, scale,
    q_in, g_in, norm_in, delta_in, k_in, v_in, lens_in,
    dq_out, dk_out, dv_out,
    qa, ga, qt, gt, kv, ka, va, dq, part, code, got, probs, grads, stat, base, ends,
    q_sem, g_sem, own_sem, kv_send, kv_recv, part_send, part_recv,
):
    heads, rows, width = dq.shape
    chunks = rows // CHUNK
    f32, b16 = jnp.float32, jnp.bfloat16
    me = lax.axis_index("dp") * sections + lax.axis_index("section")
    right = lax.rem(me + 1, count)
    left = lax.rem(me + count - 1, count)
    right = (right // sections, lax.rem(right, sections))
    left = (left // sections, lax.rem(left, sections))

    def load_q(h):
        return pltpu.make_async_copy(q_in.at[h], qa.at[h, :, pl.ds(0, width)], q_sem.at[h])

    def load_g(h):
        return pltpu.make_async_copy(g_in.at[h], ga.at[h, :, pl.ds(0, width)], g_sem.at[h])

    own = [pltpu.make_async_copy(ref, kv.at[0, j], own_sem.at[j]) for j, ref in enumerate((k_in, v_in))]
    for copy in own:
        copy.start()

    def start_loads(h, carry):
        load_q(h).start()
        load_g(h).start()
        return carry

    lax.fori_loop(0, heads, start_loads, 0)

    barrier = pltpu.get_barrier_semaphore()
    for neighbour in (left, right):
        pl.semaphore_signal(barrier, inc=1, device_id=neighbour, device_id_type=MESH)

    def pass_on(offset):
        return [
            pltpu.make_async_remote_copy(
                src_ref=(k_in, v_in)[j] if offset == 0 else kv.at[offset, j],
                dst_ref=kv.at[offset + 1, j],
                send_sem=kv_send.at[offset, j],
                recv_sem=kv_recv.at[offset, j],
                device_id=right,
                device_id_type=MESH,
            )
            for j in range(2)
        ]

    def hand_back(offset, chunk):
        return pltpu.make_async_remote_copy(
            src_ref=code.at[offset - 1, chunk],
            dst_ref=got.at[offset - 1, chunk],
            send_sem=part_send.at[offset - 1, chunk],
            recv_sem=part_recv.at[offset - 1, chunk],
            device_id=left,
            device_id_type=MESH,
        )

    pl.semaphore_wait(barrier, 2)
    for copy in pass_on(0):
        copy.start()

    line = lax.broadcasted_iota(jnp.int32, (256, 256), 0)
    lane = lax.broadcasted_iota(jnp.int32, (256, 256), 1)
    lens = lens_in[...].astype(f32)
    ends[...] = jnp.sum(jnp.where(lane <= line, lens, 0.0), axis=1, keepdims=True)
    row = lax.broadcasted_iota(jnp.int32, (width, rows), 0)
    rowf = row.astype(f32)
    place = lax.broadcasted_iota(jnp.int32, (1, rows), 1)

    def matches(offset):
        first = lax.rem(me + count - offset, count) * rows
        where = (first + place).astype(f32)
        number = jnp.sum(jnp.where(ends[...] <= where, 1.0, 0.0), axis=0, keepdims=True)
        high = jnp.floor(number * (1.0 / DIGIT))
        low = number - high * DIGIT + DIGIT
        return (rowf == high) | (rowf == low)

    def key_side(offset):
        blocked = jnp.where(matches(offset), 0.0, -MASKED)
        ones = jnp.where(row < 2 * DIGIT + 3, 1.0, 0.0)
        ka[offset, :, width:] = jnp.where(row < 2 * DIGIT, blocked, ones).astype(b16).T
        va[offset, :, width:] = jnp.where(row < 1, 1.0, 0.0).astype(b16).T

    def take_keys(offset):
        ka[offset, :, :width] = kv[offset, 0]
        va[offset, :, :width] = kv[offset, 1]

    base[...] = jnp.where(matches(0), 1.0, 0.0)
    stat[0] = norm_in[...].astype(f32) * (-1.0 / scale)
    stat[1] = -delta_in[...].astype(f32)

    def prepare(h, carry):
        norm = stat[0, pl.ds(h, 1), :]
        high = norm.astype(b16).astype(f32)
        middle = (norm - high).astype(b16).astype(f32)
        low = norm - high - middle
        extra = jnp.where(
            row == 2 * DIGIT,
            high,
            jnp.where(row == 2 * DIGIT + 1, middle, jnp.where(row == 2 * DIGIT + 2, low, base[...])),
        )
        qa[h, :, width:] = extra.astype(b16).T
        ga[h, :, width:] = jnp.where(row == 0, stat[1, pl.ds(h, 1), :], 0.0).astype(b16).T
        load_q(h).wait()
        load_g(h).wait()
        qt[h] = qa[h, :, :width].T
        gt[h] = ga[h, :, :width].T
        dq[h] = jnp.zeros((rows, width), f32)
        return carry

    lax.fori_loop(0, heads, prepare, 0)
    for offset in range(REACH + 1):
        key_side(offset)
    for copy in own:
        copy.wait()
    take_keys(0)
    part[...] = jnp.zeros_like(part)

    def first_half(offset, chunk, h, slot):
        low, high = rows_of(offset, chunk, rows)
        keys = slice(chunk * CHUNK, (chunk + 1) * CHUNK)
        scores = dot(qa[h, low:high, :], ka[offset, keys, :], NT)
        if offset == 0:
            i = lax.broadcasted_iota(jnp.int32, scores.shape, 0)
            j = lax.broadcasted_iota(jnp.int32, scores.shape, 1)
            scores = jnp.where(j <= i, scores, -1e30)
        p = jnp.exp2(scores * (scale * LOG2E))
        ds = p * dot(ga[h, low:high, :], va[offset, keys, :], NT)
        probs[slot, low:high, :] = p.astype(b16)
        grads[slot, low:high, :] = ds.astype(b16)

    def second_half(offset, chunk, h, slot):
        low, high = rows_of(offset, chunk, rows)
        keys = slice(chunk * CHUNK, (chunk + 1) * CHUNK)
        p = probs[slot, low:high, :]
        ds = grads[slot, low:high, :]
        part[offset, chunk, 0] += dot(qt[h, :, low:high], ds, NN)
        part[offset, chunk, 1] += dot(gt[h, :, low:high], p, NN)
        dq[h, low:high, :] += dot(ds, kv[offset, 0, keys, :], NN)

    def encode(slot, chunk, total):
        top = jnp.max(jnp.abs(total), axis=1, keepdims=True)
        power = jnp.ceil(jnp.log2(jnp.maximum(top, 1e-30)))
        steps = jnp.floor(total * jnp.exp2(STEPS - power) + 0.5)
        for j in range(2):
            code[slot, chunk, j * width : (j + 1) * width, :] = steps[j].astype(jnp.int32).astype(jnp.int16)
        side = lax.broadcasted_iota(jnp.int32, (16, CHUNK), 0)
        powers = jnp.where(side == 0, power[0], jnp.where(side == 1, power[1], 0.0))
        code[slot, chunk, 2 * width :, :] = powers.astype(jnp.int32).astype(jnp.int16)

    def decoded(slot, chunk):
        power = got[slot, chunk, 2 * width :, :].astype(jnp.int32).astype(f32)
        unit = jnp.exp2(power - STEPS)
        return jnp.stack([
            got[slot, chunk, j * width : (j + 1) * width, :].astype(jnp.int32).astype(f32) * unit[j : j + 1, :]
            for j in range(2)
        ])

    def act(event):
        if event[0] == "kv":
            offset = event[1]
            for copy in pass_on(offset - 1):
                copy.wait_recv()
            if offset < REACH:
                for copy in pass_on(offset):
                    copy.start()
            take_keys(offset)
        else:
            _, offset, chunk = event
            total = part[offset, chunk]
            if offset < REACH:
                hand_back(offset + 1, chunk).wait_recv()
                total += decoded(offset, chunk)
            encode(offset - 1, chunk, total)
            hand_back(offset, chunk).start()

    first_half(*ORDER[0][0], 0, 0)
    for n, (item, events) in enumerate(ORDER):
        for j in range(heads // 2):
            for event in events.get(j, ()):
                act(event)
            if item is None:
                break
            following = (*item, 2 * j + 2)
            if j == heads // 2 - 1:
                following = None if ORDER[n + 1][0] is None else (*ORDER[n + 1][0], 0)
            first_half(*item, 2 * j + 1, 1)
            second_half(*item, 2 * j, 0)
            if following is not None:
                first_half(*following, 0)
            second_half(*item, 2 * j + 1, 1)

    def finish(h, carry):
        dq_out[h] = (dq[h] * (scale * EXACT)).astype(b16)
        return carry

    lax.fori_loop(0, heads, finish, 0)
    for chunk in range(chunks):
        keys = slice(chunk * CHUNK, (chunk + 1) * CHUNK)
        hand_back(1, chunk).wait_recv()
        total = part[0, chunk] + decoded(0, chunk)
        dk_out[keys, :] = (total[0] * (scale * EXACT)).T.astype(b16)
        dv_out[keys, :] = (total[1] * EXACT).T.astype(b16)
    for offset in range(REACH):
        for copy in pass_on(offset):
            copy.wait_send()
        for chunk in range(chunks):
            hand_back(offset + 1, chunk).wait_send()


def per_device(count, sections, queries, grad_out, log_norm, row_delta, key_rows, value_rows, doc_lengths):
    heads, rows, width = queries.shape
    chunks = rows // CHUNK
    scale = 1.0 / math.sqrt(width)
    f32, b16 = jnp.float32, jnp.bfloat16
    vmem = pl.BlockSpec(memory_space=pltpu.VMEM)
    anywhere = pl.BlockSpec(memory_space=pl.ANY)
    dma = pltpu.SemaphoreType.DMA
    blocks = heads * rows * (REACH + 1 - 1) * rows
    results = pl.pallas_call(
        functools.partial(kernel, count, sections, scale),
        out_shape=(
            jax.ShapeDtypeStruct((heads, rows, width), b16),
            jax.ShapeDtypeStruct((rows, width), b16),
            jax.ShapeDtypeStruct((rows, width), b16),
        ),
        in_specs=[anywhere, anywhere, vmem, vmem, anywhere, anywhere, vmem],
        out_specs=(vmem, vmem, vmem),
        scratch_shapes=[
            pltpu.VMEM((heads, rows, 2 * width), b16),
            pltpu.VMEM((heads, rows, 2 * width), b16),
            pltpu.VMEM((heads, width, rows), b16),
            pltpu.VMEM((heads, width, rows), b16),
            pltpu.VMEM((REACH + 1, 2, rows, width), b16),
            pltpu.VMEM((REACH + 1, rows, 2 * width), b16),
            pltpu.VMEM((REACH + 1, rows, 2 * width), b16),
            pltpu.VMEM((heads, rows, width), f32),
            pltpu.VMEM((REACH + 1, chunks, 2, width, CHUNK), f32),
            pltpu.VMEM((REACH, chunks, 2 * width + 16, CHUNK), jnp.int16),
            pltpu.VMEM((REACH, chunks, 2 * width + 16, CHUNK), jnp.int16),
            pltpu.VMEM((2, rows, CHUNK), b16),
            pltpu.VMEM((2, rows, CHUNK), b16),
            pltpu.VMEM((2, heads, rows), f32),
            pltpu.VMEM((width, rows), f32),
            pltpu.VMEM((256, 1), f32),
            dma((heads,)),
            dma((heads,)),
            dma((2,)),
            dma((REACH, 2)),
            dma((REACH, 2)),
            dma((REACH, chunks)),
            dma((REACH, chunks)),
        ],
        compiler_params=pltpu.CompilerParams(
            collective_id=0, has_side_effects=True, vmem_limit_bytes=56 * 1024 * 1024
        ),
        cost_estimate=pl.CostEstimate(
            flops=10 * blocks * width, bytes_accessed=8 * heads * rows * width, transcendentals=blocks
        ),
        name="packed_attention_grads",
    )(queries, grad_out, log_norm, row_delta, key_rows, value_rows, doc_lengths.reshape(1, -1))
    return tuple(result * jnp.asarray(1.0 / EXACT, b16) for result in results)


def solution(mesh):
    placed = (
        P(None, AXES, None),
        P(None, AXES, None),
        P(None, AXES),
        P(None, AXES),
        P(AXES, None),
        P(AXES, None),
        P(),
    )
    return jax.shard_map(
        functools.partial(per_device, mesh.size, mesh.shape["section"]),
        mesh=mesh,
        in_specs=placed,
        out_specs=(P(None, AXES, None), P(AXES, None), P(AXES, None)),
        check_vma=False,
    )
```

```python
import functools
import math

import jax
import jax.numpy as jnp
from jax import lax
from jax.experimental import pallas as pl
from jax.experimental.pallas import tpu as pltpu
from jax.sharding import PartitionSpec as P

AXES = ("dp", "section")
REACH = 4
CHUNK = 256
DIGIT = 16
STEPS = 14.0
MASKED = 32768.0
LOG2E = 1.4426950408889634
MESH = pl.DeviceIdType.MESH

NN = (((1,), (0,)), ((), ()))
NT = (((1,), (1,)), ((), ()))
dot = functools.partial(lax.dot_general, preferred_element_type=jnp.float32)

ORDER = (
    ((0, 1), {2: (("kv", 1, 0),)}),
    ((1, 0), {1: (("kv", 1, 1),), 3: (("kv", 1, 2),)}),
    ((1, 1), {1: (("kv", 2, 0),), 3: (("kv", 2, 1),)}),
    ((2, 0), {1: (("kv", 2, 2),), 3: (("kv", 3, 0),)}),
    ((3, 0), {2: (("kv", 3, 1),)}),
    ((3, 1), {0: (("kv", 3, 2),), 2: (("kv", 4, 0),)}),
    ((4, 0), {0: (("kv", 4, 1),)}),
    ((4, 1), {0: (("ret", 4, 0),), 1: (("kv", 4, 2),)}),
    ((4, 2), {0: (("ret", 4, 1),), 2: (("ret", 3, 0),)}),
    ((3, 2), {0: (("ret", 4, 2),), 1: (("ret", 3, 1),), 3: (("ret", 2, 0),)}),
    ((2, 1), {1: (("ret", 3, 2),)}),
    ((2, 2), {0: (("ret", 2, 1),), 2: (("ret", 1, 0),)}),
    ((1, 2), {0: (("ret", 2, 2),), 2: (("ret", 1, 1),)}),
    ((0, 2), {}),
    ((0, 0), {1: (("ret", 1, 2),)}),
    (None, {}),
)


def rows_of(offset, chunk, rows):
    if offset == 0:
        return chunk * CHUNK, rows
    if offset == REACH:
        return 0, (chunk + 1) * CHUNK
    return 0, rows


def kernel(
    count, sections, scale,
    q_in, g_in, norm_in, delta_in, k_in, v_in, lens_in,
    dq_out, dk_out, dv_out,
    qa, ga, qt, gt, kv, ka, va, dq, part, code, got, probs, grads, stat, base, ends,
    q_sem, g_sem, own_sem, kv_send, kv_recv, part_send, part_recv,
):
    heads, rows, width = dq.shape
    chunks = rows // CHUNK
    f32, b16 = jnp.float32, jnp.bfloat16
    me = lax.axis_index("dp") * sections + lax.axis_index("section")
    right = lax.rem(me + 1, count)
    left = lax.rem(me + count - 1, count)
    right = (right // sections, lax.rem(right, sections))
    left = (left // sections, lax.rem(left, sections))

    def load_q(h):
        return pltpu.make_async_copy(q_in.at[h], qa.at[h, :, pl.ds(0, width)], q_sem.at[h])

    def load_g(h):
        return pltpu.make_async_copy(g_in.at[h], ga.at[h, :, pl.ds(0, width)], g_sem.at[h])

    own = [
        pltpu.make_async_copy(ref.at[pl.ds(chunk * CHUNK, CHUNK)], kv.at[0, chunk, j], own_sem.at[chunk, j])
        for chunk in range(chunks)
        for j, ref in enumerate((k_in, v_in))
    ]
    for copy in own:
        copy.start()

    def start_loads(h, carry):
        load_q(h).start()
        load_g(h).start()
        return carry

    lax.fori_loop(0, heads, start_loads, 0)

    barrier = pltpu.get_barrier_semaphore()
    for neighbour in (left, right):
        pl.semaphore_signal(barrier, inc=1, device_id=neighbour, device_id_type=MESH)

    def pass_on(offset, chunk):
        return pltpu.make_async_remote_copy(
            src_ref=kv.at[offset, chunk],
            dst_ref=kv.at[offset + 1, chunk],
            send_sem=kv_send.at[offset, chunk],
            recv_sem=kv_recv.at[offset, chunk],
            device_id=right,
            device_id_type=MESH,
        )

    def hand_back(offset, chunk):
        return pltpu.make_async_remote_copy(
            src_ref=code.at[offset - 1, chunk],
            dst_ref=got.at[offset - 1, chunk],
            send_sem=part_send.at[offset - 1, chunk],
            recv_sem=part_recv.at[offset - 1, chunk],
            device_id=left,
            device_id_type=MESH,
        )

    for copy in own:
        copy.wait()
    pl.semaphore_wait(barrier, 2)
    for chunk in range(chunks):
        pass_on(0, chunk).start()

    line = lax.broadcasted_iota(jnp.int32, (256, 256), 0)
    lane = lax.broadcasted_iota(jnp.int32, (256, 256), 1)
    lens = lens_in[...].astype(f32)
    ends[...] = jnp.sum(jnp.where(lane <= line, lens, 0.0), axis=1, keepdims=True)
    row = lax.broadcasted_iota(jnp.int32, (width, rows), 0)
    rowf = row.astype(f32)
    place = lax.broadcasted_iota(jnp.int32, (1, rows), 1)

    def matches(offset):
        first = lax.rem(me + count - offset, count) * rows
        where = (first + place).astype(f32)
        number = jnp.sum(jnp.where(ends[...] <= where, 1.0, 0.0), axis=0, keepdims=True)
        high = jnp.floor(number * (1.0 / DIGIT))
        low = number - high * DIGIT + DIGIT
        return (rowf == high) | (rowf == low)

    def key_side(offset):
        blocked = jnp.where(matches(offset), 0.0, -MASKED)
        ones = jnp.where(row < 2 * DIGIT + 3, 1.0, 0.0)
        ka[offset, :, width:] = jnp.where(row < 2 * DIGIT, blocked, ones).astype(b16).T
        va[offset, :, width:] = jnp.where(row < 1, 1.0, 0.0).astype(b16).T

    def take_keys(offset, chunk):
        keys = slice(chunk * CHUNK, (chunk + 1) * CHUNK)
        ka[offset, keys, :width] = kv[offset, chunk, 0]
        va[offset, keys, :width] = kv[offset, chunk, 1]

    base[...] = jnp.where(matches(0), 1.0, 0.0)
    stat[0] = norm_in[...].astype(f32) * (-1.0 / scale)
    stat[1] = -delta_in[...].astype(f32)

    def prepare(h, carry):
        norm = stat[0, pl.ds(h, 1), :]
        high = norm.astype(b16).astype(f32)
        middle = (norm - high).astype(b16).astype(f32)
        low = norm - high - middle
        extra = jnp.where(
            row == 2 * DIGIT,
            high,
            jnp.where(row == 2 * DIGIT + 1, middle, jnp.where(row == 2 * DIGIT + 2, low, base[...])),
        )
        qa[h, :, width:] = extra.astype(b16).T
        ga[h, :, width:] = jnp.where(row == 0, stat[1, pl.ds(h, 1), :], 0.0).astype(b16).T
        load_q(h).wait()
        load_g(h).wait()
        qt[h] = qa[h, :, :width].T
        gt[h] = ga[h, :, :width].T
        dq[h] = jnp.zeros((rows, width), f32)
        return carry

    lax.fori_loop(0, heads, prepare, 0)
    for offset in range(REACH + 1):
        key_side(offset)
    for chunk in range(chunks):
        take_keys(0, chunk)
    part[...] = jnp.zeros_like(part)

    def first_half(offset, chunk, h, slot):
        low, high = rows_of(offset, chunk, rows)
        keys = slice(chunk * CHUNK, (chunk + 1) * CHUNK)
        scores = dot(qa[h, low:high, :], ka[offset, keys, :], NT)
        if offset == 0:
            i = lax.broadcasted_iota(jnp.int32, scores.shape, 0)
            j = lax.broadcasted_iota(jnp.int32, scores.shape, 1)
            scores = jnp.where(j <= i, scores, -1e30)
        p = jnp.exp2(scores * (scale * LOG2E))
        ds = p * dot(ga[h, low:high, :], va[offset, keys, :], NT)
        probs[slot, low:high, :] = p.astype(b16)
        grads[slot, low:high, :] = ds.astype(b16)

    def second_half(offset, chunk, h, slot):
        low, high = rows_of(offset, chunk, rows)
        p = probs[slot, low:high, :]
        ds = grads[slot, low:high, :]
        part[offset, chunk, 0] += dot(qt[h, :, low:high], ds, NN)
        part[offset, chunk, 1] += dot(gt[h, :, low:high], p, NN)
        dq[h, low:high, :] += dot(ds, kv[offset, chunk, 0], NN)

    def encode(slot, chunk, total):
        top = jnp.max(jnp.abs(total), axis=1, keepdims=True)
        power = jnp.ceil(jnp.log2(jnp.maximum(top, 1e-30)))
        steps = jnp.floor(total * jnp.exp2(STEPS - power) + 0.5)
        for j in range(2):
            code[slot, chunk, j * width : (j + 1) * width, :] = steps[j].astype(jnp.int32).astype(jnp.int16)
        side = lax.broadcasted_iota(jnp.int32, (16, CHUNK), 0)
        powers = jnp.where(side == 0, power[0], jnp.where(side == 1, power[1], 0.0))
        code[slot, chunk, 2 * width :, :] = powers.astype(jnp.int32).astype(jnp.int16)

    def decoded(slot, chunk):
        power = got[slot, chunk, 2 * width :, :].astype(jnp.int32).astype(f32)
        unit = jnp.exp2(power - STEPS)
        return jnp.stack([
            got[slot, chunk, j * width : (j + 1) * width, :].astype(jnp.int32).astype(f32) * unit[j : j + 1, :]
            for j in range(2)
        ])

    def act(event):
        name, offset, chunk = event
        if name == "kv":
            pass_on(offset - 1, chunk).wait_recv()
            if offset < REACH:
                pass_on(offset, chunk).start()
            take_keys(offset, chunk)
        else:
            total = part[offset, chunk]
            if offset < REACH:
                hand_back(offset + 1, chunk).wait_recv()
                total += decoded(offset, chunk)
            encode(offset - 1, chunk, total)
            hand_back(offset, chunk).start()

    first_half(*ORDER[0][0], 0, 0)
    for n, (item, events) in enumerate(ORDER):
        for j in range(heads // 2):
            for event in events.get(j, ()):
                act(event)
            if item is None:
                break
            following = (*item, 2 * j + 2)
            if j == heads // 2 - 1:
                following = None if ORDER[n + 1][0] is None else (*ORDER[n + 1][0], 0)
            first_half(*item, 2 * j + 1, 1)
            second_half(*item, 2 * j, 0)
            if following is not None:
                first_half(*following, 0)
            second_half(*item, 2 * j + 1, 1)

    def finish(h, carry):
        dq_out[h] = (dq[h] * scale).astype(b16)
        return carry

    lax.fori_loop(0, heads, finish, 0)
    for chunk in range(chunks):
        keys = slice(chunk * CHUNK, (chunk + 1) * CHUNK)
        hand_back(1, chunk).wait_recv()
        total = part[0, chunk] + decoded(0, chunk)
        dk_out[keys, :] = (total[0] * scale).T.astype(b16)
        dv_out[keys, :] = total[1].T.astype(b16)
    for offset in range(REACH):
        for chunk in range(chunks):
            pass_on(offset, chunk).wait_send()
            hand_back(offset + 1, chunk).wait_send()


def per_device(count, sections, queries, grad_out, log_norm, row_delta, key_rows, value_rows, doc_lengths):
    heads, rows, width = queries.shape
    chunks = rows // CHUNK
    scale = 1.0 / math.sqrt(width)
    f32, b16 = jnp.float32, jnp.bfloat16
    vmem = pl.BlockSpec(memory_space=pltpu.VMEM)
    anywhere = pl.BlockSpec(memory_space=pl.ANY)
    dma = pltpu.SemaphoreType.DMA
    blocks = heads * rows * (REACH + 1 - 1) * rows
    return pl.pallas_call(
        functools.partial(kernel, count, sections, scale),
        out_shape=(
            jax.ShapeDtypeStruct((heads, rows, width), b16),
            jax.ShapeDtypeStruct((rows, width), b16),
            jax.ShapeDtypeStruct((rows, width), b16),
        ),
        in_specs=[anywhere, anywhere, vmem, vmem, anywhere, anywhere, vmem],
        out_specs=(vmem, vmem, vmem),
        scratch_shapes=[
            pltpu.VMEM((heads, rows, 2 * width), b16),
            pltpu.VMEM((heads, rows, 2 * width), b16),
            pltpu.VMEM((heads, width, rows), b16),
            pltpu.VMEM((heads, width, rows), b16),
            pltpu.VMEM((REACH + 1, chunks, 2, CHUNK, width), b16),
            pltpu.VMEM((REACH + 1, rows, 2 * width), b16),
            pltpu.VMEM((REACH + 1, rows, 2 * width), b16),
            pltpu.VMEM((heads, rows, width), f32),
            pltpu.VMEM((REACH + 1, chunks, 2, width, CHUNK), f32),
            pltpu.VMEM((REACH, chunks, 2 * width + 16, CHUNK), jnp.int16),
            pltpu.VMEM((REACH, chunks, 2 * width + 16, CHUNK), jnp.int16),
            pltpu.VMEM((2, rows, CHUNK), b16),
            pltpu.VMEM((2, rows, CHUNK), b16),
            pltpu.VMEM((2, heads, rows), f32),
            pltpu.VMEM((width, rows), f32),
            pltpu.VMEM((256, 1), f32),
            dma((heads,)),
            dma((heads,)),
            dma((chunks, 2)),
            dma((REACH, chunks)),
            dma((REACH, chunks)),
            dma((REACH, chunks)),
            dma((REACH, chunks)),
        ],
        compiler_params=pltpu.CompilerParams(
            collective_id=0, has_side_effects=True, vmem_limit_bytes=56 * 1024 * 1024
        ),
        cost_estimate=pl.CostEstimate(
            flops=10 * blocks * width, bytes_accessed=8 * heads * rows * width, transcendentals=blocks
        ),
        name="packed_attention_grads",
    )(queries, grad_out, log_norm, row_delta, key_rows, value_rows, doc_lengths.reshape(1, -1))


def solution(mesh):
    placed = (
        P(None, AXES, None),
        P(None, AXES, None),
        P(None, AXES),
        P(None, AXES),
        P(AXES, None),
        P(AXES, None),
        P(),
    )
    return jax.shard_map(
        functools.partial(per_device, mesh.size, mesh.shape["section"]),
        mesh=mesh,
        in_specs=placed,
        out_specs=(P(None, AXES, None), P(AXES, None), P(AXES, None)),
        check_vma=False,
    )
```

```python
import functools
import math

import jax
import jax.numpy as jnp
from jax import lax
from jax.experimental import pallas as pl
from jax.experimental.pallas import tpu as pltpu
from jax.sharding import PartitionSpec as P

AXES = ("dp", "section")
REACH = 4
CHUNK = 256
DIGIT = 16
STEPS = 14.0
MASKED = 32768.0
LOG2E = 1.4426950408889634
MESH = pl.DeviceIdType.MESH

NN = (((1,), (0,)), ((), ()))
NT = (((1,), (1,)), ((), ()))
dot = functools.partial(lax.dot_general, preferred_element_type=jnp.float32)

ORDER = (
    ((0, 2), (("kv", 1, 0),)),
    ((1, 0), (("kv", 1, 1),)),
    ((1, 1), (("kv", 1, 2), ("kv", 2, 0),)),
    ((2, 0), (("kv", 2, 1), ("kv", 2, 2),)),
    ((2, 2), (("kv", 3, 0), ("kv", 3, 1),)),
    ((3, 1), (("kv", 3, 2), ("kv", 4, 0),)),
    ((4, 0), (("kv", 4, 1),)),
    ((4, 1), (("kv", 4, 2), ("ret", 4, 0),)),
    ((4, 2), (("ret", 4, 1),)),
    ((3, 0), (("ret", 4, 2),)),
    ((3, 2), (("ret", 3, 1), ("ret", 3, 0),)),
    ((2, 1), (("ret", 3, 2),)),
    ((1, 2), (("ret", 2, 1), ("ret", 2, 0),)),
    ((0, 1), (("ret", 2, 2),)),
    ((0, 0), (("ret", 1, 1), ("ret", 1, 0),)),
    (None, (("ret", 1, 2),)),
)


def rows_of(offset, chunk, rows):
    if offset == 0:
        return chunk * CHUNK, rows
    if offset == REACH:
        return 0, (chunk + 1) * CHUNK
    return 0, rows


def kernel(
    count, sections, scale,
    q_in, g_in, norm_in, delta_in, k_in, v_in, lens_in,
    dq_out, dk_out, dv_out,
    qa, ga, qt, gt, kv, ka, va, dq, part, code, got, probs, grads, stat, base, ends,
    q_sem, g_sem, own_sem, kv_send, kv_recv, part_send, part_recv,
):
    heads, rows, width = dq.shape
    chunks = rows // CHUNK
    f32, b16 = jnp.float32, jnp.bfloat16
    me = lax.axis_index("dp") * sections + lax.axis_index("section")
    right = lax.rem(me + 1, count)
    left = lax.rem(me + count - 1, count)
    right = (right // sections, lax.rem(right, sections))
    left = (left // sections, lax.rem(left, sections))

    def load_q(h):
        return pltpu.make_async_copy(q_in.at[h], qa.at[h, :, pl.ds(0, width)], q_sem.at[h])

    def load_g(h):
        return pltpu.make_async_copy(g_in.at[h], ga.at[h, :, pl.ds(0, width)], g_sem.at[h])

    own = [
        pltpu.make_async_copy(ref.at[pl.ds(chunk * CHUNK, CHUNK)], kv.at[0, chunk, j], own_sem.at[chunk, j])
        for chunk in range(chunks)
        for j, ref in enumerate((k_in, v_in))
    ]
    for copy in own:
        copy.start()

    def start_loads(h, carry):
        load_q(h).start()
        load_g(h).start()
        return carry

    lax.fori_loop(0, heads, start_loads, 0)

    barrier = pltpu.get_barrier_semaphore()
    has_left, has_right = me > 0, me < count - 1

    @pl.when(has_left)
    def _():
        pl.semaphore_signal(barrier, inc=1, device_id=left, device_id_type=MESH)

    @pl.when(has_right)
    def _():
        pl.semaphore_signal(barrier, inc=1, device_id=right, device_id_type=MESH)

    def pass_on(offset, chunk):
        return pltpu.make_async_remote_copy(
            src_ref=kv.at[offset, chunk],
            dst_ref=kv.at[offset + 1, chunk],
            send_sem=kv_send.at[offset, chunk],
            recv_sem=kv_recv.at[offset, chunk],
            device_id=right,
            device_id_type=MESH,
        )

    def hand_back(offset, chunk):
        return pltpu.make_async_remote_copy(
            src_ref=code.at[offset - 1, chunk],
            dst_ref=got.at[offset - 1, chunk],
            send_sem=part_send.at[offset - 1, chunk],
            recv_sem=part_recv.at[offset - 1, chunk],
            device_id=left,
            device_id_type=MESH,
        )

    for copy in own:
        copy.wait()
    pl.semaphore_wait(barrier, has_left.astype(jnp.int32) + has_right.astype(jnp.int32))

    @pl.when(has_right)
    def _():
        for chunk in range(chunks):
            pass_on(0, chunk).start()

    for offset in range(1, REACH + 1):

        @pl.when(me < offset)
        def _(offset=offset):
            kv[offset] = jnp.zeros_like(kv[offset])

    @pl.when(me == count - 1)
    def _():
        got[...] = jnp.zeros_like(got)


    line = lax.broadcasted_iota(jnp.int32, (256, 256), 0)
    lane = lax.broadcasted_iota(jnp.int32, (256, 256), 1)
    lens = lens_in[...].astype(f32)
    ends[...] = jnp.sum(jnp.where(lane <= line, lens, 0.0), axis=1, keepdims=True)
    row = lax.broadcasted_iota(jnp.int32, (width, rows), 0)
    rowf = row.astype(f32)
    place = lax.broadcasted_iota(jnp.int32, (1, rows), 1)

    def matches(offset):
        first = lax.rem(me + count - offset, count) * rows
        where = (first + place).astype(f32)
        number = jnp.sum(jnp.where(ends[...] <= where, 1.0, 0.0), axis=0, keepdims=True)
        high = jnp.floor(number * (1.0 / DIGIT))
        low = number - high * DIGIT + DIGIT
        return (rowf == high) | (rowf == low)

    def key_side(offset):
        blocked = jnp.where(matches(offset), 0.0, -MASKED)
        ones = jnp.where(row < 2 * DIGIT + 3, 1.0, 0.0)
        key_part = jnp.where(row < 2 * DIGIT, blocked, ones).astype(b16).T
        value_part = jnp.where(row < 1, 1.0, 0.0).astype(b16).T
        for chunk in range(chunks):
            ka[offset, chunk, :, width:] = key_part[chunk * CHUNK : (chunk + 1) * CHUNK]
            va[offset, chunk, :, width:] = value_part[chunk * CHUNK : (chunk + 1) * CHUNK]

    def take_keys(offset, chunk):
        ka[offset, chunk, :, :width] = kv[offset, chunk, 0]
        va[offset, chunk, :, :width] = kv[offset, chunk, 1]

    base[...] = jnp.where(matches(0), 1.0, 0.0)
    stat[0] = norm_in[...].astype(f32) * (-1.0 / scale)
    stat[1] = -delta_in[...].astype(f32)

    def prepare(h, carry):
        norm = stat[0, pl.ds(h, 1), :]
        high = norm.astype(b16).astype(f32)
        middle = (norm - high).astype(b16).astype(f32)
        low = norm - high - middle
        extra = jnp.where(
            row == 2 * DIGIT,
            high,
            jnp.where(row == 2 * DIGIT + 1, middle, jnp.where(row == 2 * DIGIT + 2, low, base[...])),
        )
        qa[h, :, width:] = extra.astype(b16).T
        ga[h, :, width:] = jnp.where(row == 0, stat[1, pl.ds(h, 1), :], 0.0).astype(b16).T
        load_q(h).wait()
        load_g(h).wait()
        qt[h] = qa[h, :, :width].T
        gt[h] = ga[h, :, :width].T
        dq[h] = jnp.zeros((rows, width), f32)
        return carry

    lax.fori_loop(0, heads, prepare, 0)
    for offset in range(REACH + 1):
        key_side(offset)
    for chunk in range(chunks):
        take_keys(0, chunk)
    part[...] = jnp.zeros_like(part)

    def first_half(offset, chunk, at, h, slot):
        low, high = rows_of(offset, chunk, rows)
        scores = dot(qa[h, low:high, :], ka[at], NT)
        if offset == 0:
            i = lax.broadcasted_iota(jnp.int32, scores.shape, 0)
            j = lax.broadcasted_iota(jnp.int32, scores.shape, 1)
            scores = jnp.where(j <= i, scores, -1e30)
        p = jnp.exp2(scores * (scale * LOG2E))
        ds = p * dot(ga[h, low:high, :], va[at], NT)
        probs[slot, low:high, :] = p.astype(b16)
        grads[slot, low:high, :] = ds.astype(b16)

    def second_half(offset, chunk, at, h, slot):
        low, high = rows_of(offset, chunk, rows)
        p = probs[slot, low:high, :]
        ds = grads[slot, low:high, :]
        part[at[0], at[1], 0] += dot(qt[h, :, low:high], ds, NN)
        part[at[0], at[1], 1] += dot(gt[h, :, low:high], p, NN)
        dq[h, low:high, :] += dot(ds, kv[at[0], at[1], 0], NN)

    def encode(slot, chunk, total):
        top = jnp.max(jnp.abs(total), axis=1, keepdims=True)
        power = jnp.ceil(jnp.log2(jnp.maximum(top, 1e-30)))
        steps = jnp.floor(total * jnp.exp2(STEPS - power) + 0.5)
        for j in range(2):
            code[slot, chunk, j * width : (j + 1) * width, :] = steps[j].astype(jnp.int32).astype(jnp.int16)
        side = lax.broadcasted_iota(jnp.int32, (16, CHUNK), 0)
        powers = jnp.where(side == 0, power[0], jnp.where(side == 1, power[1], 0.0))
        code[slot, chunk, 2 * width :, :] = powers.astype(jnp.int32).astype(jnp.int16)

    def decoded(slot, chunk):
        power = got[slot, chunk, 2 * width :, :].astype(jnp.int32).astype(f32)
        unit = jnp.exp2(power - STEPS)
        return jnp.stack([
            got[slot, chunk, j * width : (j + 1) * width, :].astype(jnp.int32).astype(f32) * unit[j : j + 1, :]
            for j in range(2)
        ])

    def act(event):
        name, offset, chunk = event
        if name == "kv":

            @pl.when(me >= offset)
            def _():
                pass_on(offset - 1, chunk).wait_recv()

            if offset < REACH:

                @pl.when((me >= offset) & has_right)
                def _():
                    pass_on(offset, chunk).start()

            take_keys(offset, chunk)
        else:

            @pl.when(me >= offset)
            def _():
                total = part[offset, chunk]
                if offset < REACH:

                    @pl.when(has_right)
                    def _():
                        hand_back(offset + 1, chunk).wait_recv()

                    total += decoded(offset, chunk)
                encode(offset - 1, chunk, total)
                hand_back(offset, chunk).start()

    def like(one, other):
        return rows_of(*one, rows) == rows_of(*other, rows) and (one[0] == 0) == (other[0] == 0)

    ready = False
    n = 0
    while ORDER[n][0] is not None:
        end = n + 1
        while ORDER[end][0] is not None and like(ORDER[n][0], ORDER[end][0]):
            end += 1
        item, run = ORDER[n][0], ORDER[n:end]
        digits = [o * chunks + c for (o, c), _ in run]
        if not ready:
            for event in run[0][1]:
                act(event)
            first_half(*item, item, 0, 0)
        events_done = not ready

        def body(k, carry, run=run, item=item, digits=tuple(digits), events_done=events_done):
            for i, (_, events) in enumerate(run):
                if events and not (i == 0 and events_done):

                    @pl.when(k == i)
                    def _(events=events):
                        for event in events:
                            act(event)

            code = sum(d * 16**i for i, d in enumerate(digits))
            now = lax.rem(lax.shift_right_logical(code, 4 * k), 16)
            code = sum(d * 16**i for i, d in enumerate(digits[1:] + digits[-1:]))
            later = lax.rem(lax.shift_right_logical(code, 4 * k), 16)
            now = (now // chunks, lax.rem(now, chunks))
            later = (later // chunks, lax.rem(later, chunks))
            if len(run) == 1:
                now = item
            for h in range(heads):
                if h < heads - 1:
                    first_half(*item, now, h + 1, (h + 1) % 2)
                elif len(run) > 1:
                    first_half(*item, later, 0, 0)
                second_half(*item, now, h, h % 2)
            return carry

        if len(run) == 1:
            body(0, 0)
        else:
            lax.fori_loop(0, len(run), body, 0)
        ready = False
        n = end
    for event in ORDER[n][1]:
        act(event)

    def finish(h, carry):
        dq_out[h] = (dq[h] * scale).astype(b16)
        return carry

    lax.fori_loop(0, heads, finish, 0)
    for chunk in range(chunks):
        keys = slice(chunk * CHUNK, (chunk + 1) * CHUNK)

        @pl.when(has_right)
        def _(chunk=chunk):
            hand_back(1, chunk).wait_recv()

        total = part[0, chunk] + decoded(0, chunk)
        dk_out[keys, :] = (total[0] * scale).T.astype(b16)
        dv_out[keys, :] = total[1].T.astype(b16)
    for offset in range(REACH):

        @pl.when((me >= offset) & has_right)
        def _(offset=offset):
            for chunk in range(chunks):
                pass_on(offset, chunk).wait_send()

        @pl.when(me >= offset + 1)
        def _(offset=offset):
            for chunk in range(chunks):
                hand_back(offset + 1, chunk).wait_send()


def per_device(count, sections, queries, grad_out, log_norm, row_delta, key_rows, value_rows, doc_lengths):
    heads, rows, width = queries.shape
    chunks = rows // CHUNK
    scale = 1.0 / math.sqrt(width)
    f32, b16 = jnp.float32, jnp.bfloat16
    vmem = pl.BlockSpec(memory_space=pltpu.VMEM)
    anywhere = pl.BlockSpec(memory_space=pl.ANY)
    dma = pltpu.SemaphoreType.DMA
    blocks = heads * rows * (REACH + 1 - 1) * rows
    return pl.pallas_call(
        functools.partial(kernel, count, sections, scale),
        out_shape=(
            jax.ShapeDtypeStruct((heads, rows, width), b16),
            jax.ShapeDtypeStruct((rows, width), b16),
            jax.ShapeDtypeStruct((rows, width), b16),
        ),
        in_specs=[anywhere, anywhere, vmem, vmem, anywhere, anywhere, vmem],
        out_specs=(vmem, vmem, vmem),
        scratch_shapes=[
            pltpu.VMEM((heads, rows, 2 * width), b16),
            pltpu.VMEM((heads, rows, 2 * width), b16),
            pltpu.VMEM((heads, width, rows), b16),
            pltpu.VMEM((heads, width, rows), b16),
            pltpu.VMEM((REACH + 1, chunks, 2, CHUNK, width), b16),
            pltpu.VMEM((REACH + 1, chunks, CHUNK, 2 * width), b16),
            pltpu.VMEM((REACH + 1, chunks, CHUNK, 2 * width), b16),
            pltpu.VMEM((heads, rows, width), f32),
            pltpu.VMEM((REACH + 1, chunks, 2, width, CHUNK), f32),
            pltpu.VMEM((REACH, chunks, 2 * width + 16, CHUNK), jnp.int16),
            pltpu.VMEM((REACH, chunks, 2 * width + 16, CHUNK), jnp.int16),
            pltpu.VMEM((2, rows, CHUNK), b16),
            pltpu.VMEM((2, rows, CHUNK), b16),
            pltpu.VMEM((2, heads, rows), f32),
            pltpu.VMEM((width, rows), f32),
            pltpu.VMEM((256, 1), f32),
            dma((heads,)),
            dma((heads,)),
            dma((chunks, 2)),
            dma((REACH, chunks)),
            dma((REACH, chunks)),
            dma((REACH, chunks)),
            dma((REACH, chunks)),
        ],
        compiler_params=pltpu.CompilerParams(
            collective_id=0, has_side_effects=True, vmem_limit_bytes=40 * 1024 * 1024
        ),
        cost_estimate=pl.CostEstimate(
            flops=10 * blocks * width, bytes_accessed=8 * heads * rows * width, transcendentals=blocks
        ),
        name="packed_attention_grads",
    )(queries, grad_out, log_norm, row_delta, key_rows, value_rows, doc_lengths.reshape(1, -1))


def solution(mesh):
    placed = (
        P(None, AXES, None),
        P(None, AXES, None),
        P(None, AXES),
        P(None, AXES),
        P(AXES, None),
        P(AXES, None),
        P(),
    )
    return jax.shard_map(
        functools.partial(per_device, mesh.size, mesh.shape["section"]),
        mesh=mesh,
        in_specs=placed,
        out_specs=(P(None, AXES, None), P(AXES, None), P(AXES, None)),
        check_vma=False,
    )
```

```python
import functools
import math

import jax
import jax.numpy as jnp
from jax import lax
from jax.experimental import pallas as pl
from jax.experimental.pallas import tpu as pltpu
from jax.sharding import PartitionSpec as P

AXES = ("dp", "section")
REACH = 4
CHUNK = 256
DIGIT = 16
STEPS = 14.0
MASKED = 32768.0
LOG2E = 1.4426950408889634
MESH = pl.DeviceIdType.MESH

NN = (((1,), (0,)), ((), ()))
NT = (((1,), (1,)), ((), ()))
dot = functools.partial(lax.dot_general, preferred_element_type=jnp.float32)

ORDER = (
    ((0, 2), (("kv", 1, 0),)),
    ((1, 0), (("kv", 1, 1),)),
    ((1, 1), (("kv", 1, 2), ("kv", 2, 0),)),
    ((2, 0), (("kv", 2, 1), ("kv", 2, 2),)),
    ((2, 2), (("kv", 3, 0), ("kv", 3, 1),)),
    ((3, 1), (("kv", 3, 2), ("kv", 4, 0),)),
    ((4, 0), (("kv", 4, 1),)),
    ((4, 1), (("kv", 4, 2), ("ret", 4, 0),)),
    ((4, 2), (("ret", 4, 1),)),
    ((3, 0), (("ret", 4, 2),)),
    ((3, 2), (("ret", 3, 1), ("ret", 3, 0),)),
    ((2, 1), (("ret", 3, 2),)),
    ((1, 2), (("ret", 2, 1), ("ret", 2, 0),)),
    ((0, 1), (("ret", 2, 2),)),
    ((0, 0), (("ret", 1, 1), ("ret", 1, 0),)),
    (None, (("ret", 1, 2),)),
)


def rows_of(offset, chunk, rows):
    if offset == 0:
        return chunk * CHUNK, rows
    if offset == REACH:
        return 0, (chunk + 1) * CHUNK
    return 0, rows


def kernel(
    count, sections, scale,
    q_in, g_in, norm_in, delta_in, k_in, v_in, lens_in,
    dq_out, dk_out, dv_out,
    qa, ga, qt, gt, kv, ka, va, dq, part, code, got, probs, grads, stat, base, ends,
    norm_buf, delta_buf, lens_buf, dq_buf, q_sem, g_sem, small_sem, own_sem, kv_send, kv_recv, part_send, part_recv,
):
    heads, rows, width = dq.shape
    chunks = rows // CHUNK
    f32, b16 = jnp.float32, jnp.bfloat16
    me = lax.axis_index("dp") * sections + lax.axis_index("section")
    right = lax.rem(me + 1, count)
    left = lax.rem(me + count - 1, count)
    right = (right // sections, lax.rem(right, sections))
    left = (left // sections, lax.rem(left, sections))

    def load_q(h):
        return pltpu.make_async_copy(q_in.at[h], qa.at[h, :, pl.ds(0, width)], q_sem.at[h])

    def load_g(h):
        return pltpu.make_async_copy(g_in.at[h], ga.at[h, :, pl.ds(0, width)], g_sem.at[h])

    own = [
        pltpu.make_async_copy(ref.at[pl.ds(chunk * CHUNK, CHUNK)], kv.at[0, chunk, j], own_sem.at[chunk, j])
        for chunk in range(chunks)
        for j, ref in enumerate((k_in, v_in))
    ]
    small = [
        pltpu.make_async_copy(source, target, small_sem.at[i])
        for i, (source, target) in enumerate(((norm_in, norm_buf), (delta_in, delta_buf), (lens_in, lens_buf)))
    ]
    for copy in own + small:
        copy.start()

    def start_loads(h, carry):
        load_q(h).start()
        load_g(h).start()
        return carry

    lax.fori_loop(0, heads, start_loads, 0)

    barrier = pltpu.get_barrier_semaphore()
    has_left, has_right = me > 0, me < count - 1

    @pl.when(has_left)
    def _():
        pl.semaphore_signal(barrier, inc=1, device_id=left, device_id_type=MESH)

    @pl.when(has_right)
    def _():
        pl.semaphore_signal(barrier, inc=1, device_id=right, device_id_type=MESH)

    def pass_on(offset, chunk):
        return pltpu.make_async_remote_copy(
            src_ref=kv.at[offset, chunk],
            dst_ref=kv.at[offset + 1, chunk],
            send_sem=kv_send.at[offset, chunk],
            recv_sem=kv_recv.at[offset, chunk],
            device_id=right,
            device_id_type=MESH,
        )

    def hand_back(offset, chunk):
        return pltpu.make_async_remote_copy(
            src_ref=code.at[offset - 1, chunk],
            dst_ref=got.at[offset - 1, chunk],
            send_sem=part_send.at[offset - 1, chunk],
            recv_sem=part_recv.at[offset - 1, chunk],
            device_id=left,
            device_id_type=MESH,
        )

    for copy in own:
        copy.wait()
    pl.semaphore_wait(barrier, has_left.astype(jnp.int32) + has_right.astype(jnp.int32))

    @pl.when(has_right)
    def _():
        for chunk in range(chunks):
            pass_on(0, chunk).start()

    for offset in range(1, REACH + 1):

        @pl.when(me < offset)
        def _(offset=offset):
            kv[offset] = jnp.zeros_like(kv[offset])

    @pl.when(me == count - 1)
    def _():
        got[...] = jnp.zeros_like(got)


    line = lax.broadcasted_iota(jnp.int32, (256, 256), 0)
    lane = lax.broadcasted_iota(jnp.int32, (256, 256), 1)
    for copy in small:
        copy.wait()
    lens = lens_buf[...].astype(f32)
    ends[...] = jnp.sum(jnp.where(lane <= line, lens, 0.0), axis=1, keepdims=True)
    row = lax.broadcasted_iota(jnp.int32, (width, rows), 0)
    rowf = row.astype(f32)
    place = lax.broadcasted_iota(jnp.int32, (1, rows), 1)

    def matches(offset):
        first = lax.rem(me + count - offset, count) * rows
        where = (first + place).astype(f32)
        number = jnp.sum(jnp.where(ends[...] <= where, 1.0, 0.0), axis=0, keepdims=True)
        high = jnp.floor(number * (1.0 / DIGIT))
        low = number - high * DIGIT + DIGIT
        return (rowf == high) | (rowf == low)

    def key_side(offset):
        blocked = jnp.where(matches(offset), 0.0, -MASKED)
        ones = jnp.where(row < 2 * DIGIT + 3, 1.0, 0.0)
        key_part = jnp.where(row < 2 * DIGIT, blocked, ones).astype(b16).T
        value_part = jnp.where(row < 1, 1.0, 0.0).astype(b16).T
        for chunk in range(chunks):
            ka[offset, chunk, :, width:] = key_part[chunk * CHUNK : (chunk + 1) * CHUNK]
            va[offset, chunk, :, width:] = value_part[chunk * CHUNK : (chunk + 1) * CHUNK]

    def take_keys(offset, chunk):
        ka[offset, chunk, :, :width] = kv[offset, chunk, 0]
        va[offset, chunk, :, :width] = kv[offset, chunk, 1]

    base[...] = jnp.where(matches(0), 1.0, 0.0)
    stat[0] = norm_buf[...].astype(f32) * (-1.0 / scale)
    stat[1] = -delta_buf[...].astype(f32)

    def prepare(h, carry):
        norm = stat[0, pl.ds(h, 1), :]
        high = norm.astype(b16).astype(f32)
        middle = (norm - high).astype(b16).astype(f32)
        low = norm - high - middle
        extra = jnp.where(
            row == 2 * DIGIT,
            high,
            jnp.where(row == 2 * DIGIT + 1, middle, jnp.where(row == 2 * DIGIT + 2, low, base[...])),
        )
        qa[h, :, width:] = extra.astype(b16).T
        ga[h, :, width:] = jnp.where(row == 0, stat[1, pl.ds(h, 1), :], 0.0).astype(b16).T
        load_q(h).wait()
        load_g(h).wait()
        qt[h] = qa[h, :, :width].T
        gt[h] = ga[h, :, :width].T
        dq[h] = jnp.zeros((rows, width), f32)
        return carry

    lax.fori_loop(0, heads, prepare, 0)
    for offset in range(REACH + 1):
        key_side(offset)
    for chunk in range(chunks):
        take_keys(0, chunk)
    part[...] = jnp.zeros_like(part)

    def first_half(offset, chunk, at, h, slot):
        low, high = rows_of(offset, chunk, rows)
        scores = dot(qa[h, low:high, :], ka[at], NT)
        if offset == 0:
            i = lax.broadcasted_iota(jnp.int32, scores.shape, 0)
            j = lax.broadcasted_iota(jnp.int32, scores.shape, 1)
            scores = jnp.where(j <= i, scores, -1e30)
        p = jnp.exp2(scores * (scale * LOG2E))
        ds = p * dot(ga[h, low:high, :], va[at], NT)
        probs[slot, low:high, :] = p.astype(b16)
        grads[slot, low:high, :] = ds.astype(b16)

    def second_half(offset, chunk, at, h, slot):
        low, high = rows_of(offset, chunk, rows)
        p = probs[slot, low:high, :]
        ds = grads[slot, low:high, :]
        part[at[0], at[1], 0] += dot(qt[h, :, low:high], ds, NN)
        part[at[0], at[1], 1] += dot(gt[h, :, low:high], p, NN)
        dq[h, low:high, :] += dot(ds, kv[at[0], at[1], 0], NN)

    def encode(slot, chunk, total):
        top = jnp.max(jnp.abs(total), axis=1, keepdims=True)
        power = jnp.ceil(jnp.log2(jnp.maximum(top, 1e-30)))
        steps = jnp.floor(total * jnp.exp2(STEPS - power) + 0.5)
        for j in range(2):
            code[slot, chunk, j * width : (j + 1) * width, :] = steps[j].astype(jnp.int32).astype(jnp.int16)
        side = lax.broadcasted_iota(jnp.int32, (16, CHUNK), 0)
        powers = jnp.where(side == 0, power[0], jnp.where(side == 1, power[1], 0.0))
        code[slot, chunk, 2 * width :, :] = powers.astype(jnp.int32).astype(jnp.int16)

    def decoded(slot, chunk):
        power = got[slot, chunk, 2 * width :, :].astype(jnp.int32).astype(f32)
        unit = jnp.exp2(power - STEPS)
        return jnp.stack([
            got[slot, chunk, j * width : (j + 1) * width, :].astype(jnp.int32).astype(f32) * unit[j : j + 1, :]
            for j in range(2)
        ])

    def act(event):
        name, offset, chunk = event
        if name == "kv":

            @pl.when(me >= offset)
            def _():
                pass_on(offset - 1, chunk).wait_recv()

            if offset < REACH:

                @pl.when((me >= offset) & has_right)
                def _():
                    pass_on(offset, chunk).start()

            take_keys(offset, chunk)
        else:

            @pl.when(me >= offset)
            def _():
                total = part[offset, chunk]
                if offset < REACH:

                    @pl.when(has_right)
                    def _():
                        hand_back(offset + 1, chunk).wait_recv()

                    total += decoded(offset, chunk)
                encode(offset - 1, chunk, total)
                hand_back(offset, chunk).start()

    def like(one, other):
        return rows_of(*one, rows) == rows_of(*other, rows) and (one[0] == 0) == (other[0] == 0)

    ready = False
    n = 0
    while ORDER[n][0] is not None:
        end = n + 1
        while ORDER[end][0] is not None and like(ORDER[n][0], ORDER[end][0]):
            end += 1
        item, run = ORDER[n][0], ORDER[n:end]
        digits = [o * chunks + c for (o, c), _ in run]
        if not ready:
            for event in run[0][1]:
                act(event)
            first_half(*item, item, 0, 0)
        events_done = not ready

        def body(k, carry, run=run, item=item, digits=tuple(digits), events_done=events_done):
            for i, (_, events) in enumerate(run):
                if events and not (i == 0 and events_done):

                    @pl.when(k == i)
                    def _(events=events):
                        for event in events:
                            act(event)

            code = sum(d * 16**i for i, d in enumerate(digits))
            now = lax.rem(lax.shift_right_logical(code, 4 * k), 16)
            code = sum(d * 16**i for i, d in enumerate(digits[1:] + digits[-1:]))
            later = lax.rem(lax.shift_right_logical(code, 4 * k), 16)
            now = (now // chunks, lax.rem(now, chunks))
            later = (later // chunks, lax.rem(later, chunks))
            if len(run) == 1:
                now = item
            for h in range(heads):
                if h < heads - 1:
                    first_half(*item, now, h + 1, (h + 1) % 2)
                elif len(run) > 1:
                    first_half(*item, later, 0, 0)
                second_half(*item, now, h, h % 2)
            return carry

        if len(run) == 1:
            body(0, 0)
        else:
            lax.fori_loop(0, len(run), body, 0)
        ready = False
        n = end
    for event in ORDER[n][1]:
        act(event)

    def store(h):
        return pltpu.make_async_copy(dq_buf.at[h], dq_out.at[h], q_sem.at[h])

    def finish(h, carry):
        dq_buf[h] = (dq[h] * scale).astype(b16)
        store(h).start()
        return carry

    lax.fori_loop(0, heads, finish, 0)
    for chunk in range(chunks):
        keys = slice(chunk * CHUNK, (chunk + 1) * CHUNK)

        @pl.when(has_right)
        def _(chunk=chunk):
            hand_back(1, chunk).wait_recv()

        total = part[0, chunk] + decoded(0, chunk)
        dk_out[keys, :] = (total[0] * scale).T.astype(b16)
        dv_out[keys, :] = total[1].T.astype(b16)
    def stored(h, carry):
        store(h).wait()
        return carry

    lax.fori_loop(0, heads, stored, 0)
    for offset in range(REACH):

        @pl.when((me >= offset) & has_right)
        def _(offset=offset):
            for chunk in range(chunks):
                pass_on(offset, chunk).wait_send()

        @pl.when(me >= offset + 1)
        def _(offset=offset):
            for chunk in range(chunks):
                hand_back(offset + 1, chunk).wait_send()


def per_device(count, sections, queries, grad_out, log_norm, row_delta, key_rows, value_rows, doc_lengths):
    heads, rows, width = queries.shape
    chunks = rows // CHUNK
    scale = 1.0 / math.sqrt(width)
    f32, b16 = jnp.float32, jnp.bfloat16
    vmem = pl.BlockSpec(memory_space=pltpu.VMEM)
    dma = pltpu.SemaphoreType.DMA
    blocks = heads * rows * (REACH + 1 - 1) * rows
    return pl.pallas_call(
        functools.partial(kernel, count, sections, scale),
        out_shape=(
            jax.ShapeDtypeStruct((heads, rows, width), b16),
            jax.ShapeDtypeStruct((rows, width), b16),
            jax.ShapeDtypeStruct((rows, width), b16),
        ),
        in_specs=[pl.BlockSpec(memory_space=pl.ANY)] * 7,
        out_specs=(pl.BlockSpec(memory_space=pl.ANY), vmem, vmem),
        scratch_shapes=[
            pltpu.VMEM((heads, rows, 2 * width), b16),
            pltpu.VMEM((heads, rows, 2 * width), b16),
            pltpu.VMEM((heads, width, rows), b16),
            pltpu.VMEM((heads, width, rows), b16),
            pltpu.VMEM((REACH + 1, chunks, 2, CHUNK, width), b16),
            pltpu.VMEM((REACH + 1, chunks, CHUNK, 2 * width), b16),
            pltpu.VMEM((REACH + 1, chunks, CHUNK, 2 * width), b16),
            pltpu.VMEM((heads, rows, width), f32),
            pltpu.VMEM((REACH + 1, chunks, 2, width, CHUNK), f32),
            pltpu.VMEM((REACH, chunks, 2 * width + 16, CHUNK), jnp.int16),
            pltpu.VMEM((REACH, chunks, 2 * width + 16, CHUNK), jnp.int16),
            pltpu.VMEM((2, rows, CHUNK), b16),
            pltpu.VMEM((2, rows, CHUNK), b16),
            pltpu.VMEM((2, heads, rows), f32),
            pltpu.VMEM((width, rows), f32),
            pltpu.VMEM((256, 1), f32),
            pltpu.VMEM(log_norm.shape, b16),
            pltpu.VMEM(row_delta.shape, b16),
            pltpu.VMEM((1, doc_lengths.size), jnp.int32),
            pltpu.VMEM((heads, rows, width), b16),
            dma((heads,)),
            dma((heads,)),
            dma((3,)),
            dma((chunks, 2)),
            dma((REACH, chunks)),
            dma((REACH, chunks)),
            dma((REACH, chunks)),
            dma((REACH, chunks)),
        ],
        compiler_params=pltpu.CompilerParams(
            collective_id=0, has_side_effects=True, vmem_limit_bytes=56 * 1024 * 1024
        ),
        cost_estimate=pl.CostEstimate(
            flops=10 * blocks * width, bytes_accessed=8 * heads * rows * width, transcendentals=blocks
        ),
        name="packed_attention_grads",
    )(queries, grad_out, log_norm, row_delta, key_rows, value_rows, doc_lengths.reshape(1, -1))


def solution(mesh):
    placed = (
        P(None, AXES, None),
        P(None, AXES, None),
        P(None, AXES),
        P(None, AXES),
        P(AXES, None),
        P(AXES, None),
        P(),
    )
    return jax.shard_map(
        functools.partial(per_device, mesh.size, mesh.shape["section"]),
        mesh=mesh,
        in_specs=placed,
        out_specs=(P(None, AXES, None), P(AXES, None), P(AXES, None)),
        check_vma=False,
    )
```
